128 devices in a mesh: lat: 8 (over x, core), ord: 16 (over z, y).
Axes of the slice: x: 4, y: 4, z: 4, core: 2. Of those that a mesh axis runs over, the one named last changes fastest.
Arguments:
- residual: float32 [32, 3, 2, 64, 8192], P('ord', None, None, None, 'lat'), may hold values from -9 to 9
- direction: float32 [32, 3, 2, 64, 8192], P('ord', None, None, None, 'lat'), may hold values from -9 to 9
- legendre_zero: bfloat16 [32, 1024, 8192], P('ord', None, 'lat'), may hold values from -0.0625 to 0.0625
- legendre_plus: bfloat16 [32, 1024, 8192], P('ord', None, 'lat'), may hold values from -0.0625 to 0.0625
- legendre_minus: bfloat16 [32, 1024, 8192], P('ord', None, 'lat'), may hold values from -0.0625 to 0.0625
- order_pairs: int32 [32], replicated, may hold values from 0 to 8191, as said below
- hit_counts: int32 [1024, 16384], P(('lat', 'ord')), may hold values from 0 to 32768, as said below
- noise_weight: float32 [2], replicated, may hold values from 0.0003 to 0.0013
- prior_inverse: float32 [3, 8192], P(None, 'lat'), may hold values from 0.5 to 2
- prior_cross: float32 [8192], P('lat'), may hold values from -0.4 to 0.4
Outputs:
- residual_next: float32 [32, 3, 2, 64, 8192], P('ord', None, None, None, 'lat')
- direction_next: float32 [32, 3, 2, 64, 8192], P('ord', None, None, None, 'lat')
- step_size: float32 [64], replicated
The draws below stay inside these ranges and needn't reach their ends.
Inputs may be any that keep to these rules, and one draw needn't show every extreme that they name: `order_pairs`: all entries are distinct; entries 2i and 2i+1 are m and 8191 - m with m < 4096; 0 and 8191 occur. `hit_counts`: 0 marks an unobserved pixel.
All inputs are finite; a program needn't handle non-finite values.
Results may differ from the reference program's by a relative error of at most 0.0043.
Values may be sent and summed in bfloat16 or wider, within the bound.
A program may use at most 192 MiB of HBM per device.

```python
import math
import jax
import jax.numpy as jnp
from jax import lax

MAX_MULTIPOLE = 8192
NPHI = 16384
FIELD_IMAGES = 64
ORDERS = 32
LATITUDE_LINES = 1024


def degree_scale():
    return jnp.sqrt(1.0 + 2.0 * jnp.arange(MAX_MULTIPOLE, dtype=jnp.float32) / MAX_MULTIPOLE)


def draw_residual(key, part):
    key = jax.random.fold_in(key, 11)
    shape = (ORDERS, 3, 2, FIELD_IMAGES, MAX_MULTIPOLE)
    base = jnp.clip(jax.random.normal(key, shape, jnp.float32), -5.0, 5.0)
    return base * degree_scale()


def draw_direction(key, part):
    key = jax.random.fold_in(key, 17)
    shape = (ORDERS, 3, 2, FIELD_IMAGES, MAX_MULTIPOLE)
    base = jnp.clip(jax.random.normal(key, shape, jnp.float32), -5.0, 5.0)
    return base * degree_scale()


def draw_order_pairs(key, part):
    key = jax.random.fold_in(key, 5)
    first_key, second_key = jax.random.split(key)
    half_count = ORDERS // 2
    picks = jax.random.permutation(first_key, MAX_MULTIPOLE // 2 - 1)[:half_count - 1] + 1
    lower = jnp.concatenate([jnp.zeros((1,), jnp.int32), picks.astype(jnp.int32)])
    lower = jax.random.permutation(second_key, lower)
    return jnp.stack([lower, MAX_MULTIPOLE - 1 - lower], 1).reshape(ORDERS).astype(jnp.int32)


def draw_hit_counts(key, part):
    key = jax.random.fold_in(key, 23)
    level_key, seen_key = jax.random.split(key)
    shape = (LATITUDE_LINES, NPHI)
    levels = jax.random.randint(level_key, shape, 0, 16, dtype=jnp.int32)
    seen = jax.random.randint(seen_key, shape, 0, 4, dtype=jnp.int32) == 0
    counts = jnp.where(seen, jnp.left_shift(jnp.ones(shape, jnp.int32), levels), jnp.zeros(shape, jnp.int32))
    counts = counts.at[0, 0].set(32768)
    counts = counts.at[0, 1].set(0)
    return counts.astype(jnp.int32)


def shard_levels(own_key, dims, cuts, low, high):
    level, own = 1.0, jax.random.fold_in(own_key, 6)
    for axis_at, shards_of in cuts:
        steps = jnp.exp(jax.random.uniform(jax.random.fold_in(own, axis_at), (shards_of,), jnp.float32, low / len(cuts), high / len(cuts)))
        level = level * jnp.repeat(steps, dims[axis_at] // shards_of).reshape([-1 if axis == axis_at else 1 for axis in range(len(dims))])
    return level


def bell_draw(stream_key, extent, deviation, reach, shards=(), kind=jnp.bfloat16):
    array = jax.random.normal(stream_key, extent, jnp.float32) * deviation
    if len(shards) > 0:
        array = shard_levels(stream_key, extent, shards, -0.22, 0.18) * array
    return jnp.clip(array, min=-reach, max=reach).astype(kind)


def setup_inputs(seed: int = 0) -> dict:
    seeds = jax.random.split(jax.random.key(seed), 11)
    residual = draw_residual(jax.random.fold_in(seeds[10], 71), 0)
    direction = draw_direction(jax.random.fold_in(seeds[10], 71), 0)
    legendre_zero = bell_draw(seeds[2], (ORDERS, LATITUDE_LINES, MAX_MULTIPOLE), MAX_MULTIPOLE ** -0.5, 0.0625, ((0, 16), (2, 8)))
    legendre_plus = bell_draw(seeds[3], (ORDERS, LATITUDE_LINES, MAX_MULTIPOLE), MAX_MULTIPOLE ** -0.5, 0.0625, ((0, 16), (2, 8)))
    legendre_minus = bell_draw(seeds[4], (ORDERS, LATITUDE_LINES, MAX_MULTIPOLE), MAX_MULTIPOLE ** -0.5, 0.0625, ((0, 16), (2, 8)))
    order_pairs = draw_order_pairs(jax.random.fold_in(seeds[10], 71), 0)
    hit_counts = draw_hit_counts(jax.random.fold_in(seeds[10], 71), 0)
    noise_weight = jnp.clip(jnp.exp(jax.random.uniform(seeds[7], (2,), jnp.float32, math.log(0.0003), math.log(0.0013))), 0.0003, 0.0013)
    prior_inverse = jnp.clip(jnp.exp(math.log(2.0) - 1.3862944 * jax.random.uniform(seeds[8], (3, MAX_MULTIPOLE), jnp.float32) ** shard_levels(seeds[8], (3, MAX_MULTIPOLE), ((1, 8),), -0.2, 0.2)), 0.5, 2.0)
    prior_cross = jnp.clip(jax.random.uniform(seeds[9], (MAX_MULTIPOLE,), jnp.float32, -0.4, 0.4) * shard_levels(seeds[9], (MAX_MULTIPOLE,), ((0, 8),), -0.4, 0.0), -0.4, 0.4)
    return dict(residual=residual, direction=direction, legendre_zero=legendre_zero, legendre_plus=legendre_plus, legendre_minus=legendre_minus, order_pairs=order_pairs, hit_counts=hit_counts, noise_weight=noise_weight, prior_inverse=prior_inverse, prior_cross=prior_cross)


def cycle_table(order_values, cycle_global):
    phase_index = jnp.arange(NPHI, dtype=jnp.int32)
    orders = order_values[:, None]
    phase_units = (2 * orders * phase_index[None, :] + orders * (cycle_global % 2)) % (2 * NPHI)
    angles = jnp.pi * phase_units.astype(jnp.float32) / NPHI
    factor = jnp.where(order_values == 0, 1.0, 2.0).astype(jnp.float32)[:, None]
    phase_table = jnp.stack([factor * jnp.cos(angles), -factor * jnp.sin(angles)], 1)
    return phase_table.astype(jnp.bfloat16).reshape(2 * order_values.shape[0], NPHI)


def combine_forward_halves(intensity_field, positive_spin_field, negative_spin_field):
    leading_inphase = -positive_spin_field[..., 0, :] + negative_spin_field[..., 3, :]
    leading_quadrature = -positive_spin_field[..., 1, :] - negative_spin_field[..., 2, :]
    trailing_inphase = -positive_spin_field[..., 2, :] - negative_spin_field[..., 1, :]
    trailing_quadrature = -positive_spin_field[..., 3, :] + negative_spin_field[..., 0, :]
    return jnp.stack([intensity_field, jnp.stack([leading_inphase, leading_quadrature], -2), jnp.stack([trailing_inphase, trailing_quadrature], -2)], -3)


def combine_transpose_halves(intensity_field, positive_spin_field, negative_spin_field):
    symmetric_inphase = -positive_spin_field[..., 0, 0, :, :] + negative_spin_field[..., 1, 1, :, :]
    symmetric_quadrature = -positive_spin_field[..., 0, 1, :, :] - negative_spin_field[..., 1, 0, :, :]
    bmode_inphase = -positive_spin_field[..., 1, 0, :, :] - negative_spin_field[..., 0, 1, :, :]
    bmode_quadrature = -positive_spin_field[..., 1, 1, :, :] + negative_spin_field[..., 0, 0, :, :]
    return jnp.stack([intensity_field, jnp.stack([symmetric_inphase, symmetric_quadrature], -3), jnp.stack([bmode_inphase, bmode_quadrature], -3)], -4)


def prior_term(multipole_amplitudes, pivot_values_list, mixed_power_product):
    intensity_field = pivot_values_list[0] * multipole_amplitudes[:, 0] + mixed_power_product * multipole_amplitudes[:, 1]
    emode_field = mixed_power_product * multipole_amplitudes[:, 0] + pivot_values_list[1] * multipole_amplitudes[:, 1]
    bmode_field = pivot_values_list[2] * multipole_amplitudes[:, 2]
    return jnp.stack([intensity_field, emode_field, bmode_field], 1)


def reference(residual, direction, legendre_zero, legendre_plus, legendre_minus, order_pairs, hit_counts, noise_weight, prior_inverse, prior_cross):
    degrees = jnp.arange(MAX_MULTIPOLE, dtype=jnp.int32)
    live_mask = (degrees[None, :] >= order_pairs[:, None]).astype(jnp.float32)[:, None, None, None, :]
    current = residual * live_mask
    search = direction * live_mask
    coefs_low = search.astype(jnp.bfloat16)

    def synth_order(operands):
        axisymmetric_lookup, plus_table, minus_table, expansion_slab = operands
        intensity_field = jnp.dot(axisymmetric_lookup, expansion_slab[0].reshape(2 * FIELD_IMAGES, MAX_MULTIPOLE).T, preferred_element_type=jnp.float32)
        polar = expansion_slab[1:3].reshape(4 * FIELD_IMAGES, MAX_MULTIPOLE).T
        positive_spin_field = jnp.dot(plus_table, polar, preferred_element_type=jnp.float32)
        negative_spin_field = jnp.dot(minus_table, polar, preferred_element_type=jnp.float32)
        return combine_forward_halves(intensity_field.reshape(LATITUDE_LINES, 2, FIELD_IMAGES), positive_spin_field.reshape(LATITUDE_LINES, 4, FIELD_IMAGES), negative_spin_field.reshape(LATITUDE_LINES, 4, FIELD_IMAGES))

    phases = lax.map(synth_order, (legendre_zero, legendre_plus, legendre_minus, coefs_low))
    phases = phases.astype(jnp.bfloat16).transpose(1, 0, 2, 3, 4)
    component_weight = jnp.stack([noise_weight[0], noise_weight[1], noise_weight[1]]) * (MAX_MULTIPOLE / (LATITUDE_LINES * NPHI))

    def cycle_pass(operands):
        cycle_global, cycle_block, cycle_hits = operands
        phase_table = cycle_table(order_pairs, cycle_global)
        flattened = cycle_block.transpose(1, 3, 0, 2).reshape(3 * FIELD_IMAGES, 2 * ORDERS)
        sky_map = jnp.dot(flattened, phase_table, preferred_element_type=jnp.float32)
        weights = cycle_hits.astype(jnp.float32)[None, None, :] * component_weight[:, None, None]
        weighted = (sky_map.reshape(3, FIELD_IMAGES, NPHI) * weights).astype(jnp.bfloat16).reshape(3 * FIELD_IMAGES, NPHI)
        adjoint = jnp.dot(weighted, phase_table.T, preferred_element_type=jnp.float32).astype(jnp.bfloat16)
        return adjoint.reshape(3, FIELD_IMAGES, ORDERS, 2).transpose(2, 0, 3, 1)

    cycle_ids = jnp.arange(LATITUDE_LINES, dtype=jnp.int32)
    adjoint_phases = lax.map(cycle_pass, (cycle_ids, phases, hit_counts)).transpose(1, 0, 2, 3, 4)

    def adjoint_order(operands):
        axisymmetric_lookup, plus_table, minus_table, fourier_line_slab = operands
        intensity_field = jnp.dot(fourier_line_slab[:, 0].reshape(LATITUDE_LINES, 2 * FIELD_IMAGES).T, axisymmetric_lookup, preferred_element_type=jnp.float32)
        polar = fourier_line_slab[:, 1:3].reshape(LATITUDE_LINES, 4 * FIELD_IMAGES).T
        positive_spin_field = jnp.dot(polar, plus_table, preferred_element_type=jnp.float32)
        negative_spin_field = jnp.dot(polar, minus_table, preferred_element_type=jnp.float32)
        return combine_transpose_halves(intensity_field.reshape(2, FIELD_IMAGES, MAX_MULTIPOLE), positive_spin_field.reshape(2, 2, FIELD_IMAGES, MAX_MULTIPOLE), negative_spin_field.reshape(2, 2, FIELD_IMAGES, MAX_MULTIPOLE))

    data_term = lax.map(adjoint_order, (legendre_zero, legendre_plus, legendre_minus, adjoint_phases))
    image = live_mask * (data_term + prior_term(search, prior_inverse, prior_cross))
    sum_axes = (0, 1, 2, 4)
    norm_now = jnp.sum(current * current, axis=sum_axes)
    curvature = jnp.sum(search * image, axis=sum_axes)
    step_size = norm_now / curvature
    residual_next = current - step_size[None, None, None, :, None] * image
    norm_next = jnp.sum(residual_next * residual_next, axis=sum_axes)
    norm_ratio = norm_next / norm_now
    direction_next = residual_next + norm_ratio[None, None, None, :, None] * search
    return residual_next, direction_next, step_size
```

```python
import functools
import math

import jax
import jax.numpy as jnp
from jax import lax
from jax.experimental import pallas as pl
from jax.experimental.pallas import tpu as pltpu
from jax.sharding import PartitionSpec as P

MESH = pl.DeviceIdType.MESH
BF = jnp.bfloat16
F32 = jnp.float32
NT = (((1,), (1,)), ((), ()))

LAT = 8
ORD = 16
KM = 64
CIRC = 8
NPHI = 16384
LMAX = 8192
LINES = 1024
DEG = LMAX // LAT
CHUNKS = ((0, 1), (1, 2))
SCALE = LMAX / (LINES * NPHI)


def weight_kernel(orders, hits, g, z, w, rz, rw, lhs, rhs, acc):
    m_total = orders.shape[0]
    half = NPHI // 2
    lane = lax.broadcasted_iota(jnp.int32, (8, 128), 1)
    parity = lax.broadcasted_iota(jnp.int32, (8, 128), 0) & 1

    def seed(m, carry):
        order = orders[m]
        units = (2 * order * lane + order * parity) & (2 * NPHI - 1)
        angle = units.astype(F32) * (math.pi / NPHI)
        size = jnp.where(order == 0, 1.0, 2.0).astype(F32)
        re = size * jnp.cos(angle)
        im = -size * jnp.sin(angle)
        turn = jnp.full((8, 128), (256 * order) & (2 * NPHI - 1), jnp.int32)
        turn = turn.astype(F32) * (math.pi / NPHI)
        wre = jnp.cos(turn)
        wim = -jnp.sin(turn)
        sign = jnp.full((8, 128), 1 - 2 * (order & 1), jnp.int32).astype(F32)
        z[m, 0] = re
        z[m, 1] = im
        w[m, 0] = wre
        w[m, 1] = wim
        w[m, 2] = sign
        for par in range(2):
            rz[par, 0, pl.ds(m, 1), :] = re[par : par + 1]
            rz[par, 1, pl.ds(m, 1), :] = im[par : par + 1]
        rw[0, pl.ds(m, 1), :] = wre[:1]
        rw[1, pl.ds(m, 1), :] = wim[:1]
        rw[2, pl.ds(m, 1), :] = sign[:1]
        return carry

    lax.fori_loop(0, m_total, seed, 0)
    acc[...] = jnp.zeros_like(acc)

    def step(n, carry):
        base = pl.multiple_of(n * 512, 512)
        first = [hits[:, pl.ds(base + a * 128, 128)].astype(F32) for a in range(4)]
        second = [hits[:, pl.ds(half + base + a * 128, 128)].astype(F32) for a in range(4)]

        def pair(mm, inner):
            out = [[[], []] for _ in range(4)]
            out2 = [[[], []] for _ in range(4)]
            for q in range(2):
                m = 2 * mm + q
                re, im = z[m, 0], z[m, 1]
                wre, wim, sign = w[m, 0], w[m, 1], w[m, 2]
                for a in range(4):
                    flipped = second[a] * sign
                    out[a][0].append(re * first[a])
                    out[a][1].append(im * first[a])
                    out2[a][0].append(re * flipped)
                    out2[a][1].append(im * flipped)
                    re, im = re * wre - im * wim, re * wim + im * wre
                z[m, 0] = re
                z[m, 1] = im
            rows = pl.ds(pl.multiple_of(mm * 16, 16), 16)
            for a in range(4):
                for s in range(2):
                    lhs[s, rows, a * 128 : (a + 1) * 128] = jnp.concatenate(out[a][s], 0).astype(BF)
                    lhs[s, rows, 512 + a * 128 : 512 + (a + 1) * 128] = jnp.concatenate(
                        out2[a][s], 0
                    ).astype(BF)
            return inner

        lax.fori_loop(0, m_total // 2, pair, 0)
        wre, wim, sign = rw[0], rw[1], rw[2]
        for par in range(2):
            re, im = rz[par, 0], rz[par, 1]
            for a in range(4):
                for s, value in ((0, re), (1, im)):
                    rows = slice(par * 64 + s * 32, par * 64 + s * 32 + 32)
                    rhs[rows, a * 128 : (a + 1) * 128] = value.astype(BF)
                    rhs[rows, 512 + a * 128 : 512 + (a + 1) * 128] = (value * sign).astype(BF)
                re, im = re * wre - im * wim, re * wim + im * wre
            rz[par, 0] = re
            rz[par, 1] = im
        for s in range(2):
            acc[s] += lax.dot_general(lhs[s], rhs[...], NT, preferred_element_type=F32)
        return carry

    lax.fori_loop(0, half // 512, step, 0)

    row = lax.broadcasted_iota(jnp.int32, (256, 128), 0)
    lane_from = lax.broadcasted_iota(jnp.int32, (128, 256), 0)
    lane_to = lax.broadcasted_iota(jnp.int32, (128, 256), 1)
    keep = (lax.broadcasted_iota(jnp.int32, (256, 256), 0) & 7) == (
        lax.broadcasted_iota(jnp.int32, (256, 256), 1) & 7
    )
    for s in range(2):
        total = acc[s]
        total = jnp.where((row & 1) == 0, total, pltpu.roll(total, 64, 1)).astype(BF)
        for u in range(2):
            other = s if u == 0 else 1 - s
            spread = jnp.where(lane_from == other * 32 + lane_to // 8, 1.0, 0.0).astype(BF)
            block = jnp.dot(total, spread, preferred_element_type=F32)
            g[s * 256 : (s + 1) * 256, u * 256 : (u + 1) * 256] = jnp.where(
                keep, block, 0.0
            ).astype(BF)


def circle_weights(orders, hits):
    return pl.pallas_call(
        weight_kernel,
        out_shape=jax.ShapeDtypeStruct((512, 512), BF),
        in_specs=[
            pl.BlockSpec(memory_space=pltpu.SMEM),
            pl.BlockSpec(memory_space=pltpu.VMEM),
        ],
        out_specs=pl.BlockSpec(memory_space=pltpu.VMEM),
        scratch_shapes=[
            pltpu.VMEM((32, 2, 8, 128), F32),
            pltpu.VMEM((32, 3, 8, 128), F32),
            pltpu.VMEM((2, 2, 32, 128), F32),
            pltpu.VMEM((3, 32, 128), F32),
            pltpu.VMEM((2, 256, 1024), BF),
            pltpu.VMEM((128, 1024), BF),
            pltpu.VMEM((2, 256, 128), F32),
        ],
        compiler_params=pltpu.CompilerParams(vmem_limit_bytes=16 * 2**20),
    )(orders, hits)


def step_kernel(
    orders, noise, prior, cross, g, residual, direction, lz, lp, lm,
    image_out, scal_out,
    res_v, dir_v, lz_v, lp_v, lm_v, ct, cx, cy,
    part, prec, summed, relay, fin, phases, rbuf, adj, zbuf, wbuf, img, stat, st1, st2,
    load_sem, out_sem, pair_s, pair_r, ring_s, ring_r, a2a_s, a2a_r, ag_s, ag_r, red_s, red_r,
):
    lat = lax.axis_index("lat")
    ord_ = lax.axis_index("ord")
    x = lat // 2
    core = lat % 2
    partner = 2 * x + (1 - core)
    right = 2 * ((x + 1) % 4) + core
    left = 2 * ((x + 3) % 4) + core
    sent = []

    def remote(src, dst, ssem, rsem, **where):
        copy = pltpu.make_async_remote_copy(
            src_ref=src, dst_ref=dst, send_sem=ssem, recv_sem=rsem,
            device_id=where, device_id_type=MESH,
        )
        copy.start()
        sent.append(copy)
        return copy

    loads = {}

    def load(name, src, dst, i):
        copy = pltpu.make_async_copy(src, dst, load_sem.at[i])
        copy.start()
        loads[name] = copy

    load("dir", direction, dir_v, 0)
    for i, d in enumerate((2, 1, 3, 0)):
        rows = pl.ds(pl.multiple_of(((x + d) % 4) * 256, 256), 256)
        load(("z", d), lz.at[:, rows, :], lz_v.at[:, d], 1 + i)
    for i, d in enumerate((2, 1, 3, 0)):
        rows = pl.ds(pl.multiple_of(((x + d) % 4) * 256, 256), 256)
        load(("p", d), lp.at[:, rows, :], lp_v.at[:, d], 5 + i)
        load(("m", d), lm.at[:, rows, :], lm_v.at[:, d], 9 + i)
    load("res", residual, res_v, 13)

    barrier = pltpu.get_barrier_semaphore()

    def greet_lat(off, carry):
        pl.semaphore_signal(
            barrier, inc=1, device_id={"lat": (lat + off) % LAT}, device_id_type=MESH
        )
        return carry

    def greet_ord(off, carry):
        pl.semaphore_signal(
            barrier, inc=1, device_id={"ord": (ord_ + off) % ORD}, device_id_type=MESH
        )
        return carry

    lax.fori_loop(1, LAT, greet_lat, 0)
    lax.fori_loop(1, ORD, greet_ord, 0)

    degree = lax.broadcasted_iota(jnp.int32, (8, DEG), 1) + lat * DEG
    live = [jnp.where(degree >= orders[2 * ord_ + o], 1.0, 0.0).astype(F32) for o in range(2)]
    loads["dir"].wait()
    for o in range(2):
        mask = jnp.broadcast_to(live[o][:1], (KM, DEG))
        for s in range(2):
            rows = slice(s * KM, (s + 1) * KM)
            ct[o, rows, :] = (dir_v[o, 0, rows, :] * mask).astype(BF)
            e = (dir_v[o, 1, rows, :] * mask).astype(BF)
            b = (dir_v[o, 2, rows, :] * mask).astype(BF)
            cx[o, s * 64 : s * 64 + 64, :] = -e
            cx[o, 128 + s * 64 : 192 + s * 64, :] = -b
            if s == 0:
                cy[o, 192:256, :] = e
                cy[o, 64:128, :] = -b
            else:
                cy[o, 128:192, :] = -e
                cy[o, 0:64, :] = b

    pl.semaphore_wait(barrier, LAT + ORD - 2)

    def groups(first, second):
        both = jnp.concatenate([first.reshape(32, 8, 128), second.reshape(32, 8, 128)], 1)
        return both.astype(BF).reshape(2, 16, 16, 128)

    pairs = {}

    def synth(ch, d):
        lo, count = CHUNKS[ch]
        if ch == 0:
            loads["z", d].wait()
            got = [
                lax.dot_general(lz_v[o, d], ct[o], NT, preferred_element_type=F32) for o in range(2)
            ]
            part[d, :, 0] = groups(got[0], got[1])
        else:
            loads["p", d].wait()
            loads["m", d].wait()
            got = [
                lax.dot_general(lp_v[o, d], cx[o], NT, preferred_element_type=F32)
                + lax.dot_general(lm_v[o, d], cy[o], NT, preferred_element_type=F32)
                for o in range(2)
            ]
            part[d, :, 1] = groups(got[0][:, :128], got[1][:, :128])
            part[d, :, 2] = groups(got[0][:, 128:], got[1][:, 128:])
        cs = pl.ds(lo, count)
        pairs[ch, d] = remote(
            part.at[d, 1 - core, cs], prec.at[d, cs], pair_s.at[ch, d], pair_r.at[ch, d], lat=partner
        )

    rings = {}

    def chunk(ch):
        lo, count = CHUNKS[ch]
        return lo, count, pl.ds(lo, count), slice(lo, lo + count)

    def pair_sum(ch, d, lo_g, hi_g):
        _, _, _, c = chunk(ch)
        return part[d, core, c, lo_g:hi_g].astype(F32) + prec[d, c, lo_g:hi_g].astype(F32)

    def ring_far(ch):
        _, _, cs, c = chunk(ch)
        pairs[ch, 2].wait_recv()
        summed[2, c] = pair_sum(ch, 2, 0, 16).astype(BF)
        a, b = pl.ds(0, 8), pl.ds(8, 8)
        rings[ch, 0] = remote(
            summed.at[2, cs, a], relay.at[0, cs], ring_s.at[ch, 0], ring_r.at[ch, 0], lat=right
        )
        rings[ch, 1] = remote(
            summed.at[2, cs, b], relay.at[1, cs], ring_s.at[ch, 1], ring_r.at[ch, 1], lat=left
        )

    def ring_near(ch, d, part_no):
        _, _, cs, c = chunk(ch)
        side = 0 if d == 1 else 1
        if part_no == 0:
            pairs[ch, d].wait_recv()
            lo_g = 8 if d == 1 else 0
            summed[d, c, lo_g : lo_g + 8] = pair_sum(ch, d, lo_g, lo_g + 8).astype(BF)
        else:
            lo_g = 0 if d == 1 else 8
            rings[ch, side].wait_recv()
            summed[d, c, lo_g : lo_g + 8] = (
                pair_sum(ch, d, lo_g, lo_g + 8) + relay[side, c].astype(F32)
            ).astype(BF)
        sem = 2 + side * 2 + part_no
        span = pl.ds(lo_g, 8)
        rings[ch, sem] = remote(
            summed.at[d, cs, span], fin.at[side, cs, span], ring_s.at[ch, sem], ring_r.at[ch, sem],
            lat=right if d == 1 else left,
        )

    def ring_end(ch):
        _, _, _, c = chunk(ch)
        pairs[ch, 0].wait_recv()
        for sem in (2, 4, 3, 5):
            rings[ch, sem].wait_recv()
        phases[c] = (
            pair_sum(ch, 0, 0, 16) + fin[0, c].astype(F32) + fin[1, c].astype(F32)
        ).astype(BF)

    def exchange(ch, way, src, dst):
        lo, count, cs, c = chunk(ch)

        def copy(off):
            to = (ord_ + off) % ORD
            return pltpu.make_async_remote_copy(
                src_ref=src.at[cs, to], dst_ref=dst.at[cs, ord_],
                send_sem=a2a_s.at[way, ch, off], recv_sem=a2a_r.at[way, ch, off],
                device_id={"ord": to}, device_id_type=MESH,
            )

        def go(off, carry):
            copy(off).start()
            return carry

        def wait(off, carry):
            copy(off).wait_recv()
            return carry

        def drain(off, carry):
            copy(off).wait_send()
            return carry

        lax.fori_loop(1, ORD, go, 0)
        for i in range(lo, lo + count):
            dst[i, ord_] = src[i, ord_]
        return (
            lambda: lax.fori_loop(1, ORD, wait, 0),
            lambda: lax.fori_loop(1, ORD, drain, 0),
        )

    left_half = lax.broadcasted_iota(jnp.int32, (256, 128), 1) < KM

    def apply(ch):
        lo, count, _, _ = chunk(ch)
        for i in range(lo, lo + count):
            here = rbuf[i].reshape(256, 128)
            swapped = pltpu.roll(here.astype(F32), KM, 1).astype(BF)
            out = jnp.dot(
                g[...], jnp.concatenate([here, swapped], 0), preferred_element_type=F32
            )
            out = jnp.where(left_half, out[:256], out[256:]) * (noise[min(i, 1)] * SCALE)
            adj[i] = out.astype(BF).reshape(16, 16, 128)

    def turn(ch):
        lo, count, _, _ = chunk(ch)
        for i in range(lo, lo + count):
            got = zbuf[i].astype(F32).reshape(16, 2, 8, 128)
            for o in range(2):
                wbuf[lat, i, o] = got[:, o].reshape(128, 128).T.astype(BF)

    gathers = {}

    def gather(ch, i, slot, cs, o, **where):
        view = wbuf.at[slot, cs] if o is None else wbuf.at[slot, cs, o]
        gathers[ch, i] = remote(view, view, ag_s.at[ch, i], ag_r.at[ch, i], **where)

    def gather_start(ch):
        _, _, cs, _ = chunk(ch)
        gather(ch, 1, lat, cs, None, lat=right)
        gather(ch, 2, lat, cs, None, lat=left)
        gather(ch, 0, lat, cs, None, lat=partner)

    def gather_near(ch):
        _, _, cs, _ = chunk(ch)
        gathers[ch, 1].wait_recv()
        gather(ch, 3, left, cs, 0, lat=right)
        gather(ch, 5, left, cs, None, lat=partner)
        gathers[ch, 2].wait_recv()
        gather(ch, 4, right, cs, 1, lat=left)
        gather(ch, 6, right, cs, None, lat=partner)

    def gather_far(ch):
        _, _, cs, _ = chunk(ch)
        far = 2 * ((x + 2) % 4) + core
        gathers[ch, 3].wait_recv()
        gather(ch, 7, far, cs, 0, lat=partner)
        gathers[ch, 4].wait_recv()
        gather(ch, 8, far, cs, 1, lat=partner)

    gather_waits = {0: (0,), 3: (5,), 1: (6,), 2: (7, 8)}

    def analysis(ch, d, first):
        slot = 2 * ((x + d) % 4)
        for i in gather_waits[d]:
            gathers[ch, i].wait_recv()
        for o in range(2):
            if ch == 0:
                lhs = jnp.concatenate([wbuf[slot, 0, o], wbuf[slot + 1, 0, o]], 1)
                got = jnp.dot(lhs, lz_v[o, d], preferred_element_type=F32)
                img[o, 0] = got if first else img[o, 0] + got
            else:
                q = jnp.concatenate([wbuf[slot, 1, o], wbuf[slot + 1, 1, o]], 1)
                u = jnp.concatenate([wbuf[slot, 2, o], wbuf[slot + 1, 2, o]], 1)
                straight = jnp.concatenate([-q, -u], 0)
                crossed = jnp.concatenate([u[64:], -u[:64], -q[64:], q[:64]], 0)
                got = jnp.dot(straight, lp_v[o, d], preferred_element_type=F32) + jnp.dot(
                    crossed, lm_v[o, d], preferred_element_type=F32
                )
                for c in range(2):
                    piece = got[c * 128 : (c + 1) * 128]
                    img[o, 1 + c] = piece if first else img[o, 1 + c] + piece

    synth(0, 2)
    synth(0, 1)
    ring_far(0)
    synth(0, 3)
    ring_near(0, 1, 0)
    synth(0, 0)
    ring_near(0, 3, 0)
    ring_near(0, 1, 1)
    ring_near(0, 3, 1)
    synth(1, 2)
    synth(1, 1)
    ring_far(1)
    synth(1, 3)
    ring_near(1, 1, 0)
    synth(1, 0)
    ring_near(1, 3, 0)
    ring_end(0)
    wait_a, drain_a = exchange(0, 0, phases, rbuf)
    ring_near(1, 1, 1)
    ring_near(1, 3, 1)
    wait_a()
    apply(0)
    wait_b, drain_b = exchange(0, 1, adj, zbuf)
    ring_end(1)
    wait_c, drain_c = exchange(1, 0, phases, rbuf)
    wait_b()
    turn(0)
    gather_start(0)
    wait_c()
    apply(1)
    wait_d, drain_d = exchange(1, 1, adj, zbuf)
    gather_near(0)
    analysis(0, 0, True)
    wait_d()
    turn(1)
    gather_start(1)
    gather_far(0)
    analysis(0, 3, False)
    analysis(0, 1, False)
    analysis(0, 2, False)
    analysis(1, 0, True)
    gather_near(1)
    analysis(1, 3, False)
    analysis(1, 1, False)
    gather_far(1)
    analysis(1, 2, False)
    loads["res"].wait()

    column = lax.broadcasted_iota(jnp.int32, (8, 128), 1)
    stat[...] = jnp.zeros_like(stat)

    def finish(i, carry):
        k0 = pl.multiple_of(i * 8, 8)
        sums = [jnp.zeros((8, DEG), F32) for _ in range(4)]
        for o in range(2):
            for s in range(2):
                rows = pl.ds(s * KM + k0, 8)
                search = [dir_v[o, c, rows, :] * live[o] for c in range(3)]
                priors = (
                    prior[0:1] * search[0] + cross[...] * search[1],
                    cross[...] * search[0] + prior[1:2] * search[1],
                    prior[2:3] * search[2],
                )
                for c in range(3):
                    image = live[o] * (img[o, c, rows, :] + priors[c])
                    img[o, c, rows, :] = image
                    current = res_v[o, c, rows, :] * live[o]
                    sums[0] += current * current
                    sums[1] += search[c] * image
                    sums[2] += current * image
                    sums[3] += image * image
        tile = jnp.zeros((8, 128), F32)
        for q in range(4):
            tile = jnp.where(column == q, jnp.sum(sums[q], axis=1, keepdims=True), tile)
        stat[pl.ds(k0, 8), :] = tile
        return carry

    lax.fori_loop(0, KM // 8, finish, 0)
    store = pltpu.make_async_copy(img, image_out, out_sem)
    store.start()

    def all_reduce(buf, axis, size, me, stage):
        def copy(off):
            return pltpu.make_async_remote_copy(
                src_ref=buf.at[me], dst_ref=buf.at[me],
                send_sem=red_s.at[stage, off], recv_sem=red_r.at[stage, off],
                device_id={axis: (me + off) % size}, device_id_type=MESH,
            )

        def go(off, carry):
            copy(off).start()
            return carry

        def wait(off, carry):
            copy(off).wait()
            return carry

        lax.fori_loop(1, size, go, 0)
        lax.fori_loop(1, size, wait, 0)
        total = buf[0]
        for i in range(1, size):
            total = total + buf[i]
        return total

    st1[lat] = stat[...].T[:8]
    st2[ord_] = all_reduce(st1, "lat", LAT, lat, 0)
    total = all_reduce(st2, "ord", ORD, ord_, 1)
    norm_now, curvature, mixed, square = (total[q : q + 1] for q in range(4))
    step_size = norm_now / curvature
    norm_next = norm_now + step_size * (step_size * square - 2.0 * mixed)
    ratio = norm_next / norm_now
    sub = lax.broadcasted_iota(jnp.int32, (8, 128), 0)
    scal_out[...] = jnp.where(sub == 0, step_size, ratio)

    for drain in (drain_a, drain_b, drain_c, drain_d):
        drain()
    for copy in sent:
        copy.wait_send()
    store.wait()


def cg_sums(orders, noise, prior, cross, g, residual, direction, lz, lp, lm):
    smem = pl.BlockSpec(memory_space=pltpu.SMEM)
    vmem = pl.BlockSpec(memory_space=pltpu.VMEM)
    hbm = pl.BlockSpec(memory_space=pl.ANY)
    dma = pltpu.SemaphoreType.DMA
    nch = len(CHUNKS)
    return pl.pallas_call(
        step_kernel,
        out_shape=(
            jax.ShapeDtypeStruct((2, 3, 128, DEG), F32),
            jax.ShapeDtypeStruct((8, 128), F32),
        ),
        in_specs=[smem, smem, vmem, vmem, vmem, hbm, hbm, hbm, hbm, hbm],
        out_specs=(hbm, vmem),
        scratch_shapes=[
            pltpu.VMEM((2, 3, 128, DEG), F32),
            pltpu.VMEM((2, 3, 128, DEG), F32),
            pltpu.VMEM((2, 4, 256, DEG), BF),
            pltpu.VMEM((2, 4, 256, DEG), BF),
            pltpu.VMEM((2, 4, 256, DEG), BF),
            pltpu.VMEM((2, 128, DEG), BF),
            pltpu.VMEM((2, 256, DEG), BF),
            pltpu.VMEM((2, 256, DEG), BF),
            pltpu.VMEM((4, 2, 3, 16, 16, 128), BF),
            pltpu.VMEM((4, 3, 16, 16, 128), BF),
            pltpu.VMEM((4, 3, 16, 16, 128), BF),
            pltpu.VMEM((2, 3, 8, 16, 128), BF),
            pltpu.VMEM((2, 3, 16, 16, 128), BF),
            pltpu.VMEM((3, 16, 16, 128), BF),
            pltpu.VMEM((3, 16, 16, 128), BF),
            pltpu.VMEM((3, 16, 16, 128), BF),
            pltpu.VMEM((3, 16, 16, 128), BF),
            pltpu.VMEM((LAT, 3, 2, 128, 128), BF),
            pltpu.VMEM((2, 3, 128, DEG), F32),
            pltpu.VMEM((128, 128), F32),
            pltpu.VMEM((LAT, 8, 128), F32),
            pltpu.VMEM((ORD, 8, 128), F32),
            dma((14,)),
            dma,
            dma((nch, 4)),
            dma((nch, 4)),
            dma((nch, 6)),
            dma((nch, 6)),
            dma((2, nch, ORD)),
            dma((2, nch, ORD)),
            dma((nch, 9)),
            dma((nch, 9)),
            dma((2, ORD)),
            dma((2, ORD)),
        ],
        compiler_params=pltpu.CompilerParams(
            collective_id=0, has_side_effects=True, vmem_limit_bytes=44 * 2**20
        ),
    )(orders, noise, prior, cross, g, residual, direction, lz, lp, lm)


def per_device(
    residual,
    direction,
    legendre_zero,
    legendre_plus,
    legendre_minus,
    order_pairs,
    hit_counts,
    noise_weight,
    prior_inverse,
    prior_cross,
):
    shape = residual.shape
    flat = (2, 3, 128, DEG)
    g = circle_weights(order_pairs, hit_counts)
    image, scalars = cg_sums(
        order_pairs,
        noise_weight,
        prior_inverse,
        prior_cross.reshape(1, DEG),
        g,
        residual.reshape(flat),
        direction.reshape(flat),
        legendre_zero,
        legendre_plus,
        legendre_minus,
    )
    step_size = scalars[0, :KM]
    ratio = scalars[1, :KM]
    mine = lax.dynamic_slice_in_dim(order_pairs, lax.axis_index("ord") * 2, 2)
    degrees = lax.axis_index("lat") * DEG + jnp.arange(DEG, dtype=jnp.int32)
    live = (degrees[None, :] >= mine[:, None]).astype(F32)[:, None, None, None, :]
    residual_next = (
        residual * live - step_size[None, None, None, :, None] * image.reshape(shape)
    )
    direction_next = residual_next + ratio[None, None, None, :, None] * (direction * live)
    return residual_next, direction_next, step_size


def solution(mesh):
    coef = P("ord", None, None, None, "lat")
    table = P("ord", None, "lat")
    in_specs = (
        coef, coef, table, table, table, P(), P(("lat", "ord"), None), P(), P(None, "lat"), P("lat"),
    )
    return jax.shard_map(
        per_device, mesh=mesh, in_specs=in_specs, out_specs=(coef, coef, P()), check_vma=False
    )
```

```python
import functools
import math

import jax
import jax.numpy as jnp
from jax import lax
from jax.experimental import pallas as pl
from jax.experimental.pallas import tpu as pltpu
from jax.sharding import PartitionSpec as P

MESH = pl.DeviceIdType.MESH
BF = jnp.bfloat16
F32 = jnp.float32
NT = (((1,), (1,)), ((), ()))

LAT = 8
ORD = 16
KM = 64
CIRC = 8
NPHI = 16384
LMAX = 8192
LINES = 1024
DEG = LMAX // LAT
CHUNKS = ((0, 1), (1, 2))
AWAY = (2, 1, 3, 0)
SCALE = LMAX / (LINES * NPHI)
LIMIT_MIB = 54


def step_kernel(
    orders_h, noise_h, prior_h, cross_h, hits_h, residual, direction, lz, lp, lm,
    image_out, scal_out,
    orders, noise, prior, cross, hits, res_v, dir_v, lz_v, lp_v, lm_v, ct, cx, cy,
    own, part, prec, summed, relay, fin, phases, rbuf, adj, zbuf, wbuf, img, stat, st1, st2,
    hf, spec, base, gf, g,
    load_sem, out_sem, pair_s, pair_r, ring_s, ring_r, a2a_s, a2a_r, ag_s, ag_r, red_s, red_r,
):
    lat = lax.axis_index("lat")
    ord_ = lax.axis_index("ord")
    x = lat // 2
    core = lat % 2
    partner = 2 * x + (1 - core)
    right = 2 * ((x + 1) % 4) + core
    left = 2 * ((x + 3) % 4) + core
    sent = []

    def remote(src, dst, ssem, rsem, **where):
        copy = pltpu.make_async_remote_copy(
            src_ref=src, dst_ref=dst, send_sem=ssem, recv_sem=rsem,
            device_id=where, device_id_type=MESH,
        )
        copy.start()
        sent.append(copy)
        return copy

    loads = {}

    def load(name, src, dst):
        copy = pltpu.make_async_copy(src, dst, load_sem.at[len(loads)])
        copy.start()
        loads[name] = copy

    def table(name, src, dst, p):
        rows = pl.ds(pl.multiple_of(((x + AWAY[p]) % 4) * 256, 256), 256)
        load((name, p), src.at[:, rows, :], dst.at[:, p])

    load("orders", orders_h, orders)
    load("hits", hits_h, hits)
    load("dir_t", direction.at[:, 0], dir_v.at[:, 0])
    for p in range(4):
        table("z", lz, lz_v, p)
    load("dir_p", direction.at[:, pl.ds(1, 2)], dir_v.at[:, pl.ds(1, 2)])
    for p in range(4):
        table("p", lp, lp_v, p)
        table("m", lm, lm_v, p)
    load("noise", noise_h, noise)
    load("prior", prior_h, prior)
    load("cross", cross_h, cross)
    load("res", residual, res_v)

    barrier = pltpu.get_barrier_semaphore()

    def greet_lat(off, carry):
        pl.semaphore_signal(
            barrier, inc=1, device_id={"lat": (lat + off) % LAT}, device_id_type=MESH
        )
        return carry

    def greet_ord(off, carry):
        pl.semaphore_signal(
            barrier, inc=1, device_id={"ord": (ord_ + off) % ORD}, device_id_type=MESH
        )
        return carry

    lax.fori_loop(1, LAT, greet_lat, 0)
    lax.fori_loop(1, ORD, greet_ord, 0)

    def weight_base():
        lane = lax.broadcasted_iota(jnp.int32, (8, 128), 1)
        parity = lax.broadcasted_iota(jnp.int32, (8, 128), 0) & 1

        def body(m, carry):
            order = orders[m]
            units = (2 * order * lane + order * parity) & (2 * NPHI - 1)
            angle = units.astype(F32) * (math.pi / NPHI)
            size = jnp.where(order == 0, 1.0, 2.0).astype(F32)
            rows = pl.ds(pl.multiple_of(m * 8, 8), 8)
            base[0, rows, :] = size * jnp.cos(angle)
            base[1, rows, :] = -size * jnp.sin(angle)
            return carry

        lax.fori_loop(0, 32, body, 0)

    def weight_spectrum():
        def widen(a, carry):
            hf[pl.ds(pl.multiple_of(a * 8, 8), 8), :] = hits[
                :, pl.ds(pl.multiple_of(a * 128, 128), 128)
            ].astype(F32)
            return carry

        lax.fori_loop(0, 128, widen, 0)
        turns = (
            lax.broadcasted_iota(jnp.int32, (128, 128), 0)
            * lax.broadcasted_iota(jnp.int32, (128, 128), 1)
        ) & 127
        angle = turns.astype(F32) * (2.0 * math.pi / 128)
        wave = jnp.concatenate([jnp.cos(angle), -jnp.sin(angle)], 0)
        high = wave.astype(BF)
        low = (wave - high.astype(F32)).astype(BF)
        wave = jnp.concatenate([high, high, low, low], 1)
        for t in range(CIRC):
            line = hf[pl.ds(t, 128, stride=8), :]
            top = line.astype(BF)
            rest = (line - top.astype(F32)).astype(BF)
            out = jnp.dot(
                wave, jnp.concatenate([top, rest, top, rest], 0), preferred_element_type=F32
            )
            spec[:, t, :] = out

    def weight_rows(lo, hi, blocks):
        lane = lax.broadcasted_iota(jnp.int32, (8, 128), 1)
        diagonal = (lane & 7) == lax.broadcasted_iota(jnp.int32, (8, 128), 0)

        def body(m, carry):
            rows = pl.ds(pl.multiple_of(m * 8, 8), 8)
            re, im = base[0, rows, :], base[1, rows, :]
            order = orders[m]
            for block in range(blocks):
                tiles = [jnp.zeros((8, 128), F32) for _ in range(4)]
                for k in range(16):
                    n = block * 16 + k
                    re2, im2 = base[0, n * 8 : n * 8 + 8, :], base[1, n * 8 : n * 8 + 8, :]
                    up = (order + orders[n]) & 127
                    down = (order - orders[n]) & 127
                    up_re, up_im = spec[up], spec[128 + up]
                    down_re, down_im = spec[down], spec[128 + down]
                    rr, ii, ri, ir = re * re2, im * im2, re * im2, im * re2
                    a_re, a_im = rr - ii, ri + ir
                    b_re, b_im = rr + ii, ir - ri
                    s_re = a_re * up_re - a_im * up_im
                    s_im = a_re * up_im + a_im * up_re
                    d_re = b_re * down_re - b_im * down_im
                    d_im = b_re * down_im + b_im * down_re
                    place = diagonal & (lane // 8 == k)
                    for q, value in enumerate((d_re + s_re, s_im - d_im, s_im + d_im, d_re - s_re)):
                        value = jnp.sum(value, axis=1, keepdims=True)
                        tiles[q] = jnp.where(place, value, tiles[q])
                for q in range(4):
                    gf[q, rows, block * 128 : block * 128 + 128] = 0.5 * tiles[q]
            return carry

        lax.fori_loop(lo, hi, body, 0)

    def weight_matrix():
        for q, mirror in ((0, 0), (1, 2), (2, 1), (3, 3)):
            gf[q, 0:128, 128:256] = gf[mirror, 128:256, 0:128].T
        for s in range(2):
            for u in range(2):
                value = gf[2 * s + (s if u == 0 else 1 - s)]
                top = value.astype(BF)
                rows = slice(s * 256, s * 256 + 256)
                g[rows, u * 256 : u * 256 + 256] = top
                g[rows, 512 + u * 256 : 768 + u * 256] = (value - top.astype(F32)).astype(BF)

    def live_mask(o):
        degree = lax.broadcasted_iota(jnp.int32, (8, DEG), 1) + lat * DEG
        return jnp.where(degree >= orders[2 * ord_ + o], 1.0, 0.0).astype(F32)

    def coefs_t():
        loads["dir_t"].wait()
        for o in range(2):
            mask = jnp.broadcast_to(live_mask(o)[:1], (128, DEG))
            ct[o] = (dir_v[o, 0] * mask).astype(BF)

    def coefs_p():
        loads["dir_p"].wait()
        for o in range(2):
            mask = jnp.broadcast_to(live_mask(o)[:1], (KM, DEG))
            for s in range(2):
                rows = slice(s * KM, (s + 1) * KM)
                e = (dir_v[o, 1, rows, :] * mask).astype(BF)
                b = (dir_v[o, 2, rows, :] * mask).astype(BF)
                cx[o, s * 64 : s * 64 + 64, :] = -e
                cx[o, 128 + s * 64 : 192 + s * 64, :] = -b
                if s == 0:
                    cy[o, 192:256, :] = e
                    cy[o, 64:128, :] = -b
                else:
                    cy[o, 128:192, :] = -e
                    cy[o, 0:64, :] = b

    pairs = {}

    def keep(lo, count, c, first, second):
        both = jnp.concatenate(
            [first.reshape(32 * count, 8, 128), second.reshape(32 * count, 8, 128)], 1
        ).reshape(count, 2, 16, 16, 128)
        own[lo : lo + count, :, c] = both
        part[lo : lo + count, :, c] = both.astype(BF)

    def synth(ch, lo, count):
        c0, nc = CHUNKS[ch]
        cs = pl.ds(c0, nc)
        for p in range(lo, lo + count):
            for name in ("z",) if ch == 0 else ("p", "m"):
                loads[name, p].wait()

        def rows(ref, o):
            return ref[o, lo : lo + count].reshape(count * 256, DEG)

        if ch == 0:
            got = [
                lax.dot_general(rows(lz_v, o), ct[o], NT, preferred_element_type=F32)
                for o in range(2)
            ]
            keep(lo, count, 0, got[0], got[1])
        else:
            got = [
                lax.dot_general(rows(lp_v, o), cx[o], NT, preferred_element_type=F32)
                + lax.dot_general(rows(lm_v, o), cy[o], NT, preferred_element_type=F32)
                for o in range(2)
            ]
            keep(lo, count, 1, got[0][:, :128], got[1][:, :128])
            keep(lo, count, 2, got[0][:, 128:], got[1][:, 128:])
        for p in range(lo, lo + count):
            pairs[ch, p] = remote(
                part.at[p, 1 - core, cs], prec.at[p, cs], pair_s.at[ch, p], pair_r.at[ch, p],
                lat=partner,
            )

    rings = {}
    FAR, RIGHT, LEFT, HERE = range(4)

    def chunk(ch):
        lo, count = CHUNKS[ch]
        return lo, count, pl.ds(lo, count), slice(lo, lo + count)

    def pair_sum(ch, p, lo_g, hi_g):
        _, _, _, c = chunk(ch)
        return own[p, core, c, lo_g:hi_g] + prec[p, c, lo_g:hi_g].astype(F32)

    def ring_far(ch):
        _, _, cs, c = chunk(ch)
        pairs[ch, FAR].wait_recv()
        summed[FAR, c] = pair_sum(ch, FAR, 0, 16).astype(BF)
        a, b = pl.ds(0, 8), pl.ds(8, 8)
        rings[ch, 0] = remote(
            summed.at[FAR, cs, a], relay.at[0, cs], ring_s.at[ch, 0], ring_r.at[ch, 0], lat=right
        )
        rings[ch, 1] = remote(
            summed.at[FAR, cs, b], relay.at[1, cs], ring_s.at[ch, 1], ring_r.at[ch, 1], lat=left
        )

    def ring_near(ch, p, late):
        _, _, cs, c = chunk(ch)
        side = 0 if p == RIGHT else 1
        if late:
            lo_g = 8 * side
            rings[ch, side].wait_recv()
            value = pair_sum(ch, p, lo_g, lo_g + 8) + relay[side, c].astype(F32)
        else:
            lo_g = 8 - 8 * side
            pairs[ch, p].wait_recv()
            value = pair_sum(ch, p, lo_g, lo_g + 8)
        summed[p, c, lo_g : lo_g + 8] = value.astype(BF)
        sem = 2 + side * 2 + late
        span = pl.ds(lo_g, 8)
        rings[ch, sem] = remote(
            summed.at[p, cs, span], fin.at[side, cs, span], ring_s.at[ch, sem], ring_r.at[ch, sem],
            lat=right if p == RIGHT else left,
        )

    def ring_end(ch):
        _, _, _, c = chunk(ch)
        pairs[ch, HERE].wait_recv()
        for sem in (2, 4, 3, 5):
            rings[ch, sem].wait_recv()
        phases[c] = (
            pair_sum(ch, HERE, 0, 16) + fin[0, c].astype(F32) + fin[1, c].astype(F32)
        ).astype(BF)

    drains = []

    def exchange(ch, way, src, dst):
        lo, count, cs, _ = chunk(ch)

        def copy(off):
            to = (ord_ + off) % ORD
            return pltpu.make_async_remote_copy(
                src_ref=src.at[cs, to], dst_ref=dst.at[cs, ord_],
                send_sem=a2a_s.at[way, ch, off], recv_sem=a2a_r.at[way, ch, off],
                device_id={"ord": to}, device_id_type=MESH,
            )

        def go(off, carry):
            copy(off).start()
            return carry

        def wait(off, carry):
            copy(off).wait_recv()
            return carry

        def drain(off, carry):
            copy(off).wait_send()
            return carry

        lax.fori_loop(1, ORD, go, 0)
        for i in range(lo, lo + count):
            dst[i, ord_] = src[i, ord_]
        drains.append(lambda: lax.fori_loop(1, ORD, drain, 0))
        return lambda: lax.fori_loop(1, ORD, wait, 0)

    def apply(ch):
        lo, count, _, _ = chunk(ch)
        left_half = lax.broadcasted_iota(jnp.int32, (256, 128), 1) < KM
        columns = []
        for i in range(lo, lo + count):
            here = rbuf[i].reshape(256, 128)
            swapped = pltpu.roll(here.astype(F32), KM, 1).astype(BF)
            columns.append(jnp.concatenate([here, swapped, here, swapped], 0))
        out = jnp.dot(g[...], jnp.concatenate(columns, 1), preferred_element_type=F32)
        for n, i in enumerate(range(lo, lo + count)):
            lanes = slice(n * 128, n * 128 + 128)
            value = jnp.where(left_half, out[:256, lanes], out[256:, lanes])
            adj[i] = (value * (noise[min(i, 1)] * SCALE)).astype(BF).reshape(16, 16, 128)

    def turn(ch):
        lo, count, _, _ = chunk(ch)
        for i in range(lo, lo + count):
            got = zbuf[i].astype(F32).reshape(16, 2, 8, 128)
            for o in range(2):
                wbuf[lat, i, o] = got[:, o].reshape(128, 128).T.astype(BF)

    gathers = {}

    def gather(ch, i, slot, cs, o, **where):
        view = wbuf.at[slot, cs] if o is None else wbuf.at[slot, cs, o]
        gathers[ch, i] = remote(view, view, ag_s.at[ch, i], ag_r.at[ch, i], **where)

    def gather_start(ch):
        _, _, cs, _ = chunk(ch)
        gather(ch, 1, lat, cs, None, lat=right)
        gather(ch, 2, lat, cs, None, lat=left)
        gather(ch, 0, lat, cs, None, lat=partner)

    def gather_near(ch):
        _, _, cs, _ = chunk(ch)
        gathers[ch, 1].wait_recv()
        gather(ch, 3, left, cs, 0, lat=right)
        gather(ch, 5, left, cs, None, lat=partner)
        gathers[ch, 2].wait_recv()
        gather(ch, 4, right, cs, 1, lat=left)
        gather(ch, 6, right, cs, None, lat=partner)

    def gather_far(ch):
        _, _, cs, _ = chunk(ch)
        far = 2 * ((x + 2) % 4) + core
        gathers[ch, 3].wait_recv()
        gather(ch, 7, far, cs, 0, lat=partner)
        gathers[ch, 4].wait_recv()
        gather(ch, 8, far, cs, 1, lat=partner)

    gather_waits = {HERE: (0,), LEFT: (5,), RIGHT: (6,), FAR: (7, 8)}

    def analysis(ch, lo, count, first):
        quarters = range(lo, lo + count)
        for p in quarters:
            for i in gather_waits[p]:
                gathers[ch, i].wait_recv()
        slots = [2 * ((x + AWAY[p]) % 4) + h for p in quarters for h in range(2)]

        def lines(c, o):
            return jnp.concatenate([wbuf[slot, c, o] for slot in slots], 1)

        def rows(ref, o):
            return ref[o, lo : lo + count].reshape(count * 256, DEG)

        for o in range(2):
            if ch == 0:
                got = jnp.dot(lines(0, o), rows(lz_v, o), preferred_element_type=F32)
                img[o, 0] = got if first else img[o, 0] + got
            else:
                q, u = lines(1, o), lines(2, o)
                straight = jnp.concatenate([-q, -u], 0)
                crossed = jnp.concatenate([u[64:], -u[:64], -q[64:], q[:64]], 0)
                got = jnp.dot(straight, rows(lp_v, o), preferred_element_type=F32) + jnp.dot(
                    crossed, rows(lm_v, o), preferred_element_type=F32
                )
                for c in range(2):
                    piece = got[c * 128 : (c + 1) * 128]
                    img[o, 1 + c] = piece if first else img[o, 1 + c] + piece

    def finish(components, first):
        live = [live_mask(o) for o in range(2)]

        def body(i, carry):
            k0 = pl.multiple_of(i * 8, 8)
            sums = [None] * 4
            for o in range(2):
                for s in range(2):
                    rows = pl.ds(s * KM + k0, 8)
                    search = {}
                    for c in (0, 1) if components == (0,) else (0, 1, 2):
                        search[c] = dir_v[o, c, rows, :] * live[o]
                    for c in components:
                        if c == 0:
                            extra = prior[0:1] * search[0] + cross[...] * search[1]
                        elif c == 1:
                            extra = cross[...] * search[0] + prior[1:2] * search[1]
                        else:
                            extra = prior[2:3] * search[2]
                        image = live[o] * (img[o, c, rows, :] + extra)
                        img[o, c, rows, :] = image
                        current = res_v[o, c, rows, :] * live[o]
                        terms = (
                            current * current, search[c] * image, current * image, image * image,
                        )
                        for q in range(4):
                            part_sum = terms[q][:, :128]
                            for lane in range(128, DEG, 128):
                                part_sum = part_sum + terms[q][:, lane : lane + 128]
                            sums[q] = part_sum if sums[q] is None else sums[q] + part_sum
            for q in range(4):
                rows = pl.ds(k0, 8)
                stat[q, rows, :] = sums[q] if first else stat[q, rows, :] + sums[q]
            return carry

        lax.fori_loop(0, KM // 8, body, 0)

    stores = []

    def store(c0, nc):
        copy = pltpu.make_async_copy(
            img.at[:, pl.ds(c0, nc)], image_out.at[:, pl.ds(c0, nc)], out_sem.at[len(stores)]
        )
        copy.start()
        stores.append(copy)

    def all_reduce(buf, axis, size, me, stage):
        def copy(off):
            return pltpu.make_async_remote_copy(
                src_ref=buf.at[me], dst_ref=buf.at[me],
                send_sem=red_s.at[stage, off], recv_sem=red_r.at[stage, off],
                device_id={axis: (me + off) % size}, device_id_type=MESH,
            )

        def go(off, carry):
            copy(off).start()
            return carry

        def wait(off, carry):
            copy(off).wait_recv()
            return carry

        def drain(off, carry):
            copy(off).wait_send()
            return carry

        lax.fori_loop(1, size, go, 0)
        drains.append(lambda: lax.fori_loop(1, size, drain, 0))
        lax.fori_loop(1, size, wait, 0)
        total = buf[0]
        for i in range(1, size):
            total = total + buf[i]
        return total

    loads["orders"].wait()
    weight_base()
    loads["hits"].wait()
    weight_spectrum()
    coefs_t()
    pl.semaphore_wait(barrier, LAT + ORD - 2)
    synth(0, 0, 4)
    coefs_p()
    ring_far(0)
    ring_near(0, RIGHT, 0)
    ring_near(0, LEFT, 0)
    synth(1, 0, 2)
    ring_near(0, RIGHT, 1)
    ring_near(0, LEFT, 1)
    synth(1, 2, 2)
    ring_far(1)
    ring_near(1, RIGHT, 0)
    ring_near(1, LEFT, 0)
    ring_end(0)
    wait_a = exchange(0, 0, phases, rbuf)
    weight_rows(0, 16, 1)
    ring_near(1, RIGHT, 1)
    ring_near(1, LEFT, 1)
    weight_rows(16, 32, 2)
    weight_matrix()
    loads["noise"].wait()
    wait_a()
    apply(0)
    wait_b = exchange(0, 1, adj, zbuf)
    ring_end(1)
    wait_c = exchange(1, 0, phases, rbuf)
    wait_b()
    turn(0)
    gather_start(0)
    wait_c()
    apply(1)
    wait_d = exchange(1, 1, adj, zbuf)
    gather_near(0)
    analysis(0, HERE, 1, True)
    wait_d()
    turn(1)
    gather_start(1)
    gather_far(0)
    analysis(0, RIGHT, 2, False)
    analysis(0, FAR, 1, False)
    gather_near(1)
    for name in ("prior", "cross", "res"):
        loads[name].wait()
    finish((0,), True)
    store(0, 1)
    analysis(1, HERE, 1, True)
    gather_far(1)
    analysis(1, RIGHT, 2, False)
    analysis(1, FAR, 1, False)
    finish((1, 2), False)
    store(1, 2)

    column = lax.broadcasted_iota(jnp.int32, (KM, 128), 1)
    tile = jnp.zeros((KM, 128), F32)
    for q in range(4):
        tile = jnp.where(column == q, jnp.sum(stat[q], axis=1, keepdims=True), tile)
    st1[lat] = jnp.concatenate([tile, tile], 0).T[:8]
    st2[ord_] = all_reduce(st1, "lat", LAT, lat, 0)
    total = all_reduce(st2, "ord", ORD, ord_, 1)
    norm_now, curvature, mixed, square = (total[q : q + 1] for q in range(4))
    step_size = norm_now / curvature
    norm_next = norm_now + step_size * (step_size * square - 2.0 * mixed)
    ratio = norm_next / norm_now
    sub = lax.broadcasted_iota(jnp.int32, (8, 128), 0)
    rows = jnp.where(sub == 0, step_size, ratio)
    for o in range(2):
        start = (orders[2 * ord_ + o] - lat * DEG).astype(F32)
        rows = jnp.where(sub == 2 + o, start, rows)
    scal_out[...] = rows

    for drain in drains:
        drain()
    for copy in sent:
        copy.wait_send()
    for copy in stores:
        copy.wait()


def cg_sums(*operands):
    vmem = pl.BlockSpec(memory_space=pltpu.VMEM)
    hbm = pl.BlockSpec(memory_space=pltpu.HBM)
    dma = pltpu.SemaphoreType.DMA
    nch = len(CHUNKS)
    return pl.pallas_call(
        step_kernel,
        out_shape=(
            jax.ShapeDtypeStruct((2, 3, 128, DEG), F32),
            jax.ShapeDtypeStruct((8, 128), F32),
        ),
        in_specs=[hbm] * 10,
        out_specs=(pl.BlockSpec(memory_space=pl.ANY), vmem),
        scratch_shapes=[
            pltpu.SMEM((32,), jnp.int32),
            pltpu.SMEM((2,), F32),
            pltpu.VMEM((3, DEG), F32),
            pltpu.VMEM((1, DEG), F32),
            pltpu.VMEM((CIRC, NPHI), jnp.int32),
            pltpu.VMEM((2, 3, 128, DEG), F32),
            pltpu.VMEM((2, 3, 128, DEG), F32),
            pltpu.VMEM((2, 4, 256, DEG), BF),
            pltpu.VMEM((2, 4, 256, DEG), BF),
            pltpu.VMEM((2, 4, 256, DEG), BF),
            pltpu.VMEM((2, 128, DEG), BF),
            pltpu.VMEM((2, 256, DEG), BF),
            pltpu.VMEM((2, 256, DEG), BF),
            pltpu.VMEM((4, 2, 3, 16, 16, 128), F32),
            pltpu.VMEM((4, 2, 3, 16, 16, 128), BF),
            pltpu.VMEM((4, 3, 16, 16, 128), BF),
            pltpu.VMEM((4, 3, 16, 16, 128), BF),
            pltpu.VMEM((2, 3, 8, 16, 128), BF),
            pltpu.VMEM((2, 3, 16, 16, 128), BF),
            pltpu.VMEM((3, 16, 16, 128), BF),
            pltpu.VMEM((3, 16, 16, 128), BF),
            pltpu.VMEM((3, 16, 16, 128), BF),
            pltpu.VMEM((3, 16, 16, 128), BF),
            pltpu.VMEM((LAT, 3, 2, 128, 128), BF),
            pltpu.VMEM((2, 3, 128, DEG), F32),
            pltpu.VMEM((4, KM, 128), F32),
            pltpu.VMEM((LAT, 8, 128), F32),
            pltpu.VMEM((ORD, 8, 128), F32),
            pltpu.VMEM((128 * CIRC, 128), F32),
            pltpu.VMEM((256, CIRC, 128), F32),
            pltpu.VMEM((2, 256, 128), F32),
            pltpu.VMEM((4, 256, 256), F32),
            pltpu.VMEM((512, 1024), BF),
            dma((20,)),
            dma((2,)),
            dma((nch, 4)),
            dma((nch, 4)),
            dma((nch, 6)),
            dma((nch, 6)),
            dma((2, nch, ORD)),
            dma((2, nch, ORD)),
            dma((nch, 9)),
            dma((nch, 9)),
            dma((2, ORD)),
            dma((2, ORD)),
        ],
        compiler_params=pltpu.CompilerParams(
            collective_id=0, has_side_effects=True, vmem_limit_bytes=LIMIT_MIB * 2**20
        ),
    )(*operands)


def per_device(
    residual,
    direction,
    legendre_zero,
    legendre_plus,
    legendre_minus,
    order_pairs,
    hit_counts,
    noise_weight,
    prior_inverse,
    prior_cross,
):
    shape = residual.shape
    flat = (2, 3, 128, DEG)
    image, scalars = cg_sums(
        order_pairs,
        noise_weight,
        prior_inverse,
        prior_cross.reshape(1, DEG),
        hit_counts,
        residual.reshape(flat),
        direction.reshape(flat),
        legendre_zero,
        legendre_plus,
        legendre_minus,
    )
    step_size = scalars[0, :KM]
    ratio = scalars[1, :KM]
    start = scalars[2:4, 0]
    live = (jnp.arange(DEG, dtype=F32)[None, :] >= start[:, None]).astype(F32)
    live = live[:, None, None, None, :]
    residual_next = (
        residual * live - step_size[None, None, None, :, None] * image.reshape(shape)
    )
    direction_next = residual_next + ratio[None, None, None, :, None] * (direction * live)
    return residual_next, direction_next, step_size


def solution(mesh):
    coef = P("ord", None, None, None, "lat")
    table = P("ord", None, "lat")
    in_specs = (
        coef, coef, table, table, table, P(), P(("lat", "ord"), None), P(), P(None, "lat"), P("lat"),
    )
    return jax.shard_map(
        per_device, mesh=mesh, in_specs=in_specs, out_specs=(coef, coef, P()), check_vma=False
    )
```
